512 devices in a mesh: tm: 64 (over y_hi, z, core), space: 8 (over y_lo, x).
Axes of the slice: x: 4, y: 4 (y_hi: 2, y_lo: 2; y = y_hi * 2 + y_lo), z: 16, core: 2. Of those that a mesh axis runs over, the one named last changes fastest.
Arguments:
- snapshots: float32 [64, 2, 1024, 1024], P('tm', None, 'space'), may hold values from 0.5 to 8
- coefficients: float32 [2, 1024, 1024], P(None, 'space'), may hold values from 0.9 to 1.8
Outputs:
- u_scale: float32 [64, 2, 1024, 1024], P('tm', None, 'space')
- v_scale: float32 [64, 2, 1024, 1024], P('tm', None, 'space')
The draws below stay inside these ranges and needn't reach their ends.
All inputs are finite; a program needn't handle non-finite values.
Results may differ from the reference program's by a relative error of at most 0.00002.
Values sent between devices are 32-bit elements; how exact they have to be, the bound alone decides.
A program may use at most 64 MiB of HBM per device.

```python
import math
import jax
import jax.numpy as jnp
from jax import lax

NPL = 2
ROWS = 1024
COLS = 1024
PASSES = 4
ITERS = 2
SNAPS = 64


def draw_snapshots(key, part):
    key = jax.random.fold_in(key, 11)
    layer_key, grain_key = jax.random.split(key)
    layer_shape = (SNAPS, 1, ROWS, 1)
    full_shape = (SNAPS, NPL, ROWS, COLS)
    layers = jnp.exp(jax.random.uniform(layer_key, layer_shape, jnp.float32, 0.0, math.log(8.0)))
    grain_part = jnp.exp(jax.random.uniform(grain_key, full_shape, jnp.float32, math.log(0.5), 0.0))
    return (layers * grain_part).astype(jnp.float32)


def draw_coefficients(key, part):
    key = jax.random.fold_in(key, 23)
    full_shape = (NPL, ROWS, COLS)
    return jnp.exp(jax.random.uniform(key, full_shape, jnp.float32, math.log(0.9), math.log(1.8)))


def setup_inputs(seed: int = 0) -> dict:
    splits = jax.random.split(jax.random.key(seed), 3)
    snapshots = draw_snapshots(jax.random.fold_in(splits[2], 71), 0)
    coefficients = draw_coefficients(jax.random.fold_in(splits[2], 71), 0)
    return dict(snapshots=snapshots, coefficients=coefficients)


tau_rows = 0.25
tau_side = 0.125


def row_pass(values, coef_field):
    coef_pad = jnp.pad(coef_field, ((0, 0), (1, 1), (0, 0)))
    value_pad = jnp.pad(values, ((0, 0), (1, 1), (0, 0)))
    flux_sum = 0.5 * (coef_field + coef_pad[:, 2:]) * (value_pad[:, 2:] - values)
    flux_sum = flux_sum + 0.5 * (coef_field + coef_pad[:, :-2]) * (value_pad[:, :-2] - values)
    return values + tau_rows * flux_sum


def side_pass(values, coef_field):
    coef_pad = jnp.pad(coef_field, ((1, 1), (0, 0), (1, 1)))
    value_pad = jnp.pad(values, ((1, 1), (0, 0), (1, 1)))
    flux_sum = 0.5 * (coef_field + coef_pad[2:, :, 1:-1]) * (value_pad[2:, :, 1:-1] - values)
    flux_sum = flux_sum + 0.5 * (coef_field + coef_pad[:-2, :, 1:-1]) * (value_pad[:-2, :, 1:-1] - values)
    flux_sum = flux_sum + 0.5 * (coef_field + coef_pad[1:-1, :, 2:]) * (value_pad[1:-1, :, 2:] - values)
    flux_sum = flux_sum + 0.5 * (coef_field + coef_pad[1:-1, :, :-2]) * (value_pad[1:-1, :, :-2] - values)
    return values + tau_side * flux_sum


def diffuse(values, coef_field):
    for pass_idx in range(PASSES):
        if pass_idx % 4 in (0, 3):
            values = row_pass(values, coef_field)
        else:
            values = side_pass(values, coef_field)
    return values


def reference(snapshots, coefficients):
    following = jnp.roll(snapshots, -1, axis=0)

    def solve_pair(pair_data):
        source, target = pair_data
        v_part = jnp.ones_like(source)
        u_part = jnp.ones_like(source)
        for iter_idx in range(ITERS):
            u_part = source / diffuse(v_part, coefficients)
            v_part = target / diffuse(u_part, coefficients)
        return u_part, v_part

    u_scale, v_scale = lax.map(solve_pair, (snapshots, following))
    return u_scale, v_scale
```

```python
import jax
import jax.numpy as jnp
from jax import lax
from jax.experimental import pallas as pl
from jax.experimental.pallas import tpu as pltpu
from jax.sharding import PartitionSpec as P

MESH = pl.DeviceIdType.MESH
TILE = 8
LANES = 128
CHUNK_TILES = 2


def body(
    tm, space, snap, coef, u_out, v_out, a_ext, b_ext, c_ext, vals, mids, mids2, recip, g_row, g_col, g_pl, keep, loc_sem, snd, rcv
):
    t, s = lax.axis_index("tm"), lax.axis_index("space")
    ahead, behind = lax.rem(t + 1, tm), lax.rem(t + tm - 1, tm)
    has_up, has_dn = s > 0, s < space - 1
    up, dn = jnp.maximum(s - 1, 0), jnp.minimum(s + 1, space - 1)
    height, width = coef.shape[1], coef.shape[2]
    cols = width // LANES
    tiles = height // TILE + 2
    chunks = height // (TILE * CHUNK_TILES)
    rows = TILE * CHUNK_TILES

    load_a = pltpu.make_async_copy(snap.at[0], a_ext.at[:, pl.ds(TILE, height)], loc_sem.at[0])
    load_c = pltpu.make_async_copy(coef, c_ext.at[:, pl.ds(TILE, height)], loc_sem.at[1])
    load_c.start()
    load_a.start()

    barrier = pltpu.get_barrier_semaphore()

    def greet(dst_t, dst_s):
        pl.semaphore_signal(barrier, inc=1, device_id={"tm": dst_t, "space": dst_s}, device_id_type=MESH)

    greet(ahead, s)

    @pl.when(has_up)
    def _():
        greet(t, up)
        greet(ahead, up)

    @pl.when(has_dn)
    def _():
        greet(t, dn)
        greet(ahead, dn)

    pl.semaphore_wait(barrier, 1 + 2 * has_up.astype(jnp.int32) + 2 * has_dn.astype(jnp.int32))

    def send(i, src, dst, dst_t, dst_s):
        return pltpu.make_async_remote_copy(
            src_ref=src,
            dst_ref=dst,
            send_sem=snd.at[i],
            recv_sem=rcv.at[i],
            device_id={"tm": dst_t, "space": dst_s},
            device_id_type=MESH,
        )

    first, last = pl.ds(0, TILE), pl.ds(height - TILE, TILE)
    head, tail = pl.ds(0, TILE), pl.ds(height + TILE, TILE)
    to_up = [
        send(0, coef.at[:, first], c_ext.at[:, tail], t, up),
        send(1, snap.at[0, :, first], a_ext.at[:, tail], t, up),
        send(2, snap.at[0, :, first], b_ext.at[:, tail], behind, up),
    ]
    to_dn = [
        send(3, coef.at[:, last], c_ext.at[:, head], t, dn),
        send(4, snap.at[0, :, last], a_ext.at[:, head], t, dn),
        send(5, snap.at[0, :, last], b_ext.at[:, head], behind, dn),
    ]
    for n in range(3):

        @pl.when(has_up)
        def _():
            to_up[n].start()

        @pl.when(has_dn)
        def _():
            to_dn[n].start()

    def whole(k):
        return send(
            6 + k,
            snap.at[0, :, pl.ds(k * rows, rows)],
            b_ext.at[:, pl.ds(TILE + k * rows, rows)],
            behind,
            s,
        )

    for k in range(chunks):
        whole(k).start()

    lane = lax.broadcasted_iota(jnp.int32, (TILE, LANES), 1)
    is_first, is_last = lane == 0, lane == LANES - 1

    def at(e, shift=0):
        return pl.ds(TILE * e + TILE + shift, TILE)

    def native(e, j):
        return pl.ds(pl.multiple_of(TILE * e, TILE), TILE), pl.ds(LANES * j, LANES)

    def clear(ref, e):
        for p in range(2):
            for j in range(cols):
                ref[p, j, pl.ds(TILE * e + TILE, TILE), :] = jnp.zeros((TILE, LANES), jnp.float32)

    def clear_ends(ref, lo, hi):
        @pl.when(jnp.logical_and(s == 0, lo == 0))
        def _():
            clear(ref, 0)

        @pl.when(jnp.logical_and(s == space - 1, hi == tiles))
        def _():
            clear(ref, tiles - 1)

    def row_pass(src, p, j, e):
        mid = src[p, j, at(e), :]
        below = g_row[p, j, at(e), :] * (src[p, j, at(e, 1), :] - mid)
        above = g_row[p, j, at(e, -1), :] * (mid - src[p, j, at(e, -1), :])
        return mid + (below - above)

    def side_pass(x, e):
        across = [g_pl[j, at(e), :] * (x[1][j] - x[0][j]) for j in range(cols)]
        out = []
        for p in range(2):
            rolled = [
                pltpu.roll(jnp.where(is_first, x[p][(j + 1) % cols], x[p][j]), LANES - 1, 1) for j in range(cols)
            ]
            flux = [g_col[p, j, at(e), :] * (rolled[j] - x[p][j]) for j in range(cols)]
            back = [pltpu.roll(jnp.where(is_last, flux[j - 1], flux[j]), 1, 1) for j in range(cols)]
            out.append(
                [
                    keep[p, j, at(e), :] * x[p][j] + (flux[j] - back[j]) + (across[j] if p == 0 else -across[j])
                    for j in range(cols)
                ]
            )
        return out

    def first_three(src, dst, lo, hi):
        @pl.loop(lo, hi)
        def _(e):
            x = [[row_pass(src, p, j, e) for j in range(cols)] for p in range(2)]
            x = side_pass(side_pass(x, e), e)
            for p in range(2):
                for j in range(cols):
                    dst[p, j, at(e), :] = x[p][j]

        clear_ends(dst, lo, hi)

    def fourth(src, lo, hi, put):
        @pl.loop(lo, hi)
        def _(e):
            for p in range(2):
                for j in range(cols):
                    put(p, j, e, row_pass(src, p, j, e))

    load_c.wait()

    @pl.when(has_up)
    def _():
        to_dn[0].wait_recv()

    @pl.when(has_dn)
    def _():
        to_up[0].wait_recv()

    @pl.when(s == 0)
    def _():
        c_ext[:, pl.ds(0, TILE), :] = jnp.zeros((2, TILE, width), jnp.float32)

    @pl.when(s == space - 1)
    def _():
        c_ext[:, pl.ds(height + TILE, TILE), :] = jnp.zeros((2, TILE, width), jnp.float32)

    @pl.loop(0, tiles)
    def _(e):
        for p in range(2):
            for j in range(cols):
                g_row[p, j, at(e), :] = c_ext[p, native(e, j)[0], native(e, j)[1]]
                vals[p, j, at(e), :] = jnp.ones((TILE, LANES), jnp.float32)

    clear_ends(vals, 0, tiles)

    @pl.loop(0, tiles)
    def _(e):
        c = [[g_row[p, j, at(e), :] for j in range(cols)] for p in range(2)]
        for j in range(cols):
            g_pl[j, at(e), :] = 0.0625 * (c[0][j] + c[1][j])
        for p in range(2):
            for j in range(cols):
                right = pltpu.roll(jnp.where(is_first, c[p][(j + 1) % cols], c[p][j]), LANES - 1, 1)
                side = 0.0625 * (c[p][j] + right)
                walls = 0.0625 * c[p][j]
                kept = 1.0 - walls
                if j == cols - 1:
                    side = jnp.where(is_last, 0.0, side)
                    kept = jnp.where(is_last, kept - walls, kept)
                if j == 0:
                    kept = jnp.where(is_first, kept - walls, kept)
                g_col[p, j, at(e), :] = side
                keep[p, j, at(e), :] = kept
                g_row[p, j, at(e), :] = 0.125 * (c[p][j] + g_row[p, j, at(e, 1), :])

    first_three(vals, mids, 0, tiles)
    load_a.wait()

    @pl.when(has_up)
    def _():
        to_dn[1].wait_recv()

    @pl.when(has_dn)
    def _():
        to_up[1].wait_recv()

    def put_u(p, j, e, den):
        r, c = native(e, j)
        vals[p, j, at(e), :] = a_ext[p, r, c] / den

    fourth(mids, 0, tiles, put_u)
    clear_ends(vals, 0, tiles)

    first_three(vals, mids, 0, tiles)

    def put_recip(p, j, e, den):
        recip[p, j, at(e), :] = 1.0 / den

    fourth(mids, 0, tiles, put_recip)

    @pl.when(has_up)
    def _():
        to_dn[2].wait_recv()

    @pl.when(has_dn)
    def _():
        to_up[2].wait_recv()

    def put_u_out(p, j, e, den):
        r, c = native(e, j)
        u = a_ext[p, r, c] / den
        vals[p, j, at(e), :] = u
        u_out[p, r, c] = u

    def put_v_out(p, j, e, den):
        r, c = native(e, j)
        v_out[p, r, c] = b_ext[p, r, c] / den

    def bounds(k, stage):
        low = 1 if stage == 4 else 0
        top = tiles - 1 if stage == 4 else tiles

        def reach(n):
            return jnp.where(n == chunks - 1, top, jnp.maximum(low, CHUNK_TILES * n + CHUNK_TILES + 1 - stage))

        return jnp.where(k == 0, low, reach(k - 1)), reach(k)

    @pl.loop(0, chunks)
    def _(k):
        whole(k).wait_recv()

        lo, hi = bounds(k, 0)

        @pl.loop(lo, hi)
        def _(e):
            for p in range(2):
                for j in range(cols):
                    r, c = native(e, j)
                    recip[p, j, at(e), :] = b_ext[p, r, c] * recip[p, j, at(e), :]

        clear_ends(recip, lo, hi)
        first_three(recip, mids, *bounds(k, 1))
        lo, hi = bounds(k, 2)
        fourth(mids, lo, hi, put_u_out)
        clear_ends(vals, lo, hi)
        first_three(vals, mids2, *bounds(k, 3))
        fourth(mids2, *bounds(k, 4), put_v_out)

    @pl.when(has_up)
    def _():
        for c in to_up:
            c.wait_send()

    @pl.when(has_dn)
    def _():
        for c in to_dn:
            c.wait_send()

    for k in range(chunks):
        whole(k).wait_send()


def per_device(snapshots, coefficients):
    tm, space = lax.axis_size("tm"), lax.axis_size("space")
    planes, height, width = coefficients.shape
    cols = width // LANES
    chunks = height // (TILE * CHUNK_TILES)
    wide = (planes, height + 2 * TILE, width)
    field = pltpu.VMEM((planes, cols, height + 4 * TILE, LANES), jnp.float32)
    copies = 6 + chunks

    def kernel(*refs):
        body(tm, space, *refs)

    u, v = pl.pallas_call(
        kernel,
        out_shape=[jax.ShapeDtypeStruct(wide, jnp.float32)] * 2,
        in_specs=[pl.BlockSpec(memory_space=pltpu.HBM)] * 2,
        out_specs=[pl.BlockSpec(memory_space=pltpu.VMEM)] * 2,
        scratch_shapes=[pltpu.VMEM(wide, jnp.float32)] * 3
        + [field] * 6
        + [pltpu.VMEM((cols, height + 4 * TILE, LANES), jnp.float32), field]
        + [pltpu.SemaphoreType.DMA((2,)), pltpu.SemaphoreType.DMA((copies,)), pltpu.SemaphoreType.DMA((copies,))],
        compiler_params=pltpu.CompilerParams(collective_id=0, has_side_effects=True, vmem_limit_bytes=61 * 2**20),
        name="sinkhorn",
    )(snapshots, coefficients)
    inner = slice(TILE, TILE + height)
    return u[None, :, inner], v[None, :, inner]


def solution(mesh):
    placed = (P("tm", None, "space", None), P(None, "space", None))
    return jax.shard_map(
        per_device,
        mesh=mesh,
        in_specs=placed,
        out_specs=(P("tm", None, "space", None), P("tm", None, "space", None)),
        check_vma=False,
    )
```

```python
import jax
import jax.numpy as jnp
from jax import lax
from jax.experimental import pallas as pl
from jax.experimental.pallas import tpu as pltpu
from jax.sharding import PartitionSpec as P

MESH = pl.DeviceIdType.MESH
TILE = 8
LANES = 128
PAD = 2 * TILE
GROUP = 3
SPAN = GROUP * TILE
TAU_ROWS = 0.25
TAU_SIDE = 0.125


def body(
    tm,
    space,
    snap,
    coef,
    u_out,
    v_out,
    a_ext,
    b_ext,
    c_ext,
    c_str,
    a_str,
    b_str,
    ones,
    first_u,
    first_v,
    second_u,
    second_v,
    mid_a,
    mid_b,
    recip,
    g_row,
    g_right,
    g_left,
    keep,
    g_pl,
    loc_sem,
    snd,
    rcv,
):
    t, s = lax.axis_index("tm"), lax.axis_index("space")
    ahead, behind = lax.rem(t + 1, tm), lax.rem(t + tm - 1, tm)
    has_up, has_dn = s > 0, s < space - 1
    up, dn = jnp.maximum(s - 1, 0), jnp.minimum(s + 1, space - 1)
    height, width = coef.shape[1], coef.shape[2]
    cols = width // LANES
    tiles = height // TILE + 2
    steps = tiles // GROUP
    both = [(p, j) for p in range(2) for j in range(cols)]

    load_c = pltpu.make_async_copy(coef, c_ext.at[:, pl.ds(TILE, height)], loc_sem.at[0])
    load_a = pltpu.make_async_copy(snap.at[0], a_ext.at[:, pl.ds(TILE, height)], loc_sem.at[1])
    load_c.start()
    load_a.start()

    barrier = pltpu.get_barrier_semaphore()

    def greet(dst_t, dst_s):
        pl.semaphore_signal(barrier, inc=1, device_id={"tm": dst_t, "space": dst_s}, device_id_type=MESH)

    greet(ahead, s)

    @pl.when(has_up)
    def _():
        greet(t, up)
        greet(ahead, up)

    @pl.when(has_dn)
    def _():
        greet(t, dn)
        greet(ahead, dn)

    pl.semaphore_wait(barrier, 1 + 2 * has_up.astype(jnp.int32) + 2 * has_dn.astype(jnp.int32))

    def send(i, src, dst, dst_t, dst_s):
        return pltpu.make_async_remote_copy(
            src_ref=src,
            dst_ref=dst,
            send_sem=snd.at[i],
            recv_sem=rcv.at[i],
            device_id={"tm": dst_t, "space": dst_s},
            device_id_type=MESH,
        )

    first, last = pl.ds(0, TILE), pl.ds(height - TILE, TILE)
    head, tail = pl.ds(0, TILE), pl.ds(height + TILE, TILE)
    to_up = [
        send(0, coef.at[:, first], c_ext.at[:, tail], t, up),
        send(1, snap.at[0, :, first], a_ext.at[:, tail], t, up),
        send(2, snap.at[0, :, first], b_ext.at[:, tail], behind, up),
    ]
    to_dn = [
        send(3, coef.at[:, last], c_ext.at[:, head], t, dn),
        send(4, snap.at[0, :, last], a_ext.at[:, head], t, dn),
        send(5, snap.at[0, :, last], b_ext.at[:, head], behind, dn),
    ]

    def part(k, size):
        return send(
            6 + k, snap.at[0, :, pl.ds(k * SPAN, size)], b_ext.at[:, pl.ds(k * SPAN + TILE, size)], behind, s
        )

    parts = [part(k, min(SPAN, height - k * SPAN)) for k in range(steps)]
    for n in range(3):

        @pl.when(has_up)
        def _():
            to_up[n].start()

        @pl.when(has_dn)
        def _():
            to_dn[n].start()

    for copy in parts:
        copy.start()

    def halo_arrived(n):
        @pl.when(has_up)
        def _():
            to_dn[n].wait_recv()

        @pl.when(has_dn)
        def _():
            to_up[n].wait_recv()

    lane = lax.broadcasted_iota(jnp.int32, (TILE, LANES), 1)
    is_first, is_last = lane == 0, lane == LANES - 1
    zeros = jnp.zeros((TILE, LANES), jnp.float32)

    def at(row, shift=0):
        return pl.ds(row + (PAD + shift), TILE)

    def tile(e):
        return pl.ds(pl.multiple_of(TILE * e, TILE), TILE)

    def clear_top(ref):
        @pl.when(jnp.logical_not(has_up))
        def _():
            for p, j in both:
                ref[p, j, at(0), :] = zeros

    def clear_end(ref):
        @pl.when(jnp.logical_not(has_dn))
        def _():
            for p, j in both:
                ref[p, j, at(height + TILE), :] = zeros

    def from_right(x, j):
        return pltpu.roll(jnp.where(is_first, x[(j + 1) % cols], x[j]), LANES - 1, 1)

    def from_left(x, j):
        return pltpu.roll(jnp.where(is_last, x[j - 1], x[j]), 1, 1)

    def row_pass(src, p, j, row):
        mid = src[p, j, at(row), :]
        below = g_row[p, j, at(row), :] * (src[p, j, at(row, 1), :] - mid)
        above = g_row[p, j, at(row, -1), :] * (mid - src[p, j, at(row, -1), :])
        return mid + (below - above)

    def side_pass(x, row):
        out = []
        for p in range(2):
            right = [from_right(x[p], j) for j in range(cols)]
            left = [from_left(x[p], j) for j in range(cols)]
            out.append(
                [
                    (keep[p, j, at(row), :] * x[p][j] + g_pl[j, at(row), :] * x[1 - p][j])
                    + (g_right[p, j, at(row), :] * right[j] + g_left[p, j, at(row), :] * left[j])
                    for j in range(cols)
                ]
            )
        return out

    def first_three(src, dst, row, n=GROUP):
        rows = [row + TILE * i for i in range(n)]
        x = [[[row_pass(src, p, j, r) for j in range(cols)] for p in range(2)] for r in rows]
        x = [side_pass(y, r) for y, r in zip(x, rows)]
        x = [side_pass(y, r) for y, r in zip(x, rows)]
        for y, r in zip(x, rows):
            for p, j in both:
                dst[p, j, at(r), :] = y[p][j]

    def fourth(src, num, dst, row, n=GROUP):
        for i in range(n):
            r = row + TILE * i
            for p, j in both:
                den = row_pass(src, p, j, r)
                dst[p, j, at(r), :] = (1.0 if num is None else num[p, j, at(r), :]) / den

    def strip(src, dst, e):
        for p, j in both:
            dst[p, j, at(TILE * e), :] = src[p, tile(e), pl.ds(LANES * j, LANES)]

    def weigh(e):
        row = TILE * e
        c = [[c_str[p, j, at(row), :] for j in range(cols)] for p in range(2)]
        for j in range(cols):
            g_pl[j, at(row), :] = (0.5 * TAU_SIDE) * (c[0][j] + c[1][j])
        for p in range(2):
            walls = [(0.5 * TAU_SIDE) * c[p][j] for j in range(cols)]
            right = [walls[j] + from_right(walls, j) for j in range(cols)]
            right[-1] = jnp.where(is_last, 0.0, right[-1])
            for j in range(cols):
                left = from_left(right, j)
                kept = 1.0 - walls[j] - (0.5 * TAU_SIDE) * (c[0][j] + c[1][j]) - right[j] - left
                if j == 0:
                    kept = jnp.where(is_first, kept - walls[j], kept)
                if j == cols - 1:
                    kept = jnp.where(is_last, kept - walls[j], kept)
                g_right[p, j, at(row), :] = right[j]
                g_left[p, j, at(row), :] = left
                keep[p, j, at(row), :] = kept
                g_row[p, j, at(row), :] = (0.5 * TAU_ROWS) * (c[p][j] + c_str[p, j, at(row, 1), :])

    @pl.loop(0, tiles)
    def _(e):
        for p, j in both:
            ones[p, j, at(TILE * e), :] = zeros + 1.0

    clear_top(ones)
    clear_end(ones)
    load_c.wait()

    @pl.loop(1, tiles - 1)
    def _(e):
        strip(c_ext, c_str, e)

    @pl.loop(1, tiles - 1, unroll=2)
    def _(e):
        weigh(e)

    inner = steps - 1
    gap = (tiles * TILE - inner * SPAN) // 2

    @pl.loop(0, inner)
    def _(g):
        first_three(ones, mid_a, gap + SPAN * g)

    load_a.wait()

    @pl.loop(1, tiles - 1)
    def _(e):
        strip(a_ext, a_str, e)

    halo_arrived(0)

    @pl.when(jnp.logical_not(has_up))
    def _():
        c_ext[:, head, :] = jnp.zeros((2, TILE, width), jnp.float32)

    @pl.when(jnp.logical_not(has_dn))
    def _():
        c_ext[:, tail, :] = jnp.zeros((2, TILE, width), jnp.float32)

    for e in (0, tiles - 1):
        strip(c_ext, c_str, e)
    for e in (0, tiles - 2, tiles - 1):
        weigh(e)
    first_three(ones, mid_a, gap - SPAN)
    first_three(ones, mid_a, tiles * TILE - gap)
    clear_top(mid_a)
    clear_end(mid_a)
    halo_arrived(1)
    for e in (0, tiles - 1):
        strip(a_ext, a_str, e)

    @pl.loop(0, steps)
    def _(g):
        fourth(mid_a, a_str, first_u, SPAN * g)

    clear_top(first_u)
    clear_end(first_u)

    @pl.loop(0, steps)
    def _(g):
        first_three(first_u, mid_b, SPAN * g)

    clear_top(mid_b)
    clear_end(mid_b)

    @pl.loop(0, steps)
    def _(g):
        fourth(mid_b, None, recip, SPAN * g)

    def scale(e, n):
        for i in range(n):
            for p, j in both:
                b = b_ext[p, tile(e + i), pl.ds(LANES * j, LANES)]
                b_str[p, j, at(TILE * (e + i)), :] = b
                first_v[p, j, at(TILE * (e + i)), :] = b * recip[p, j, at(TILE * (e + i)), :]

    def give(e, n):
        for i in range(n):
            for p, j in both:
                where = pl.ds(pl.multiple_of(TILE * (e + i - 1), TILE), TILE), pl.ds(LANES * j, LANES)
                u_out[0, p, where[0], where[1]] = second_u[p, j, at(TILE * (e + i)), :]
                v_out[0, p, where[0], where[1]] = second_v[p, j, at(TILE * (e + i)), :]

    def trail(end, n, clear):
        first_three(first_v, mid_a, end + 3 - TILE * n, n)
        clear(mid_a)
        fourth(mid_a, a_str, second_u, end + 2 - SPAN)
        clear(second_u)
        first_three(second_u, mid_b, end + 1 - SPAN)
        clear(mid_b)
        fourth(mid_b, b_str, second_v, end - SPAN)

    def step(e, n, end, out, n_out, clear):
        scale(e, n)
        clear(first_v)
        trail(end, n, clear)
        give(out, n_out)

    halo_arrived(2)
    parts[0].wait_recv()
    step(0, GROUP + 1, SPAN + 4, 1, GROUP - 1, clear_top)

    @pl.loop(1, steps - 1)
    def _(k):
        part(k, SPAN).wait_recv()
        step(GROUP * k + 1, GROUP, SPAN * k + (SPAN + 4), GROUP * k, GROUP, lambda ref: None)

    parts[-1].wait_recv()
    step(tiles - GROUP, GROUP, height + TILE, tiles - GROUP - 1, GROUP, clear_end)

    @pl.when(has_up)
    def _():
        for copy in to_up:
            copy.wait_send()

    @pl.when(has_dn)
    def _():
        for copy in to_dn:
            copy.wait_send()

    for copy in parts:
        copy.wait_send()


def per_device(snapshots, coefficients):
    tm, space = lax.axis_size("tm"), lax.axis_size("space")
    planes, height, width = coefficients.shape
    cols = width // LANES
    rows = height + 2 * TILE
    wide = (planes, rows, width)
    field = pltpu.VMEM((planes, cols, rows + 2 * PAD, LANES), jnp.float32)
    copies = 6 + rows // SPAN

    def kernel(*refs):
        body(tm, space, *refs)

    return pl.pallas_call(
        kernel,
        out_shape=[jax.ShapeDtypeStruct(snapshots.shape, jnp.float32)] * 2,
        in_specs=[pl.BlockSpec(memory_space=pltpu.HBM)] * 2,
        out_specs=[pl.BlockSpec(memory_space=pltpu.VMEM)] * 2,
        scratch_shapes=[pltpu.VMEM(wide, jnp.float32)] * 3
        + [field] * 15
        + [pltpu.VMEM((cols, rows + 2 * PAD, LANES), jnp.float32)]
        + [pltpu.SemaphoreType.DMA((2,)), pltpu.SemaphoreType.DMA((copies,)), pltpu.SemaphoreType.DMA((copies,))],
        compiler_params=pltpu.CompilerParams(collective_id=0, has_side_effects=True, vmem_limit_bytes=60 * 2**20),
        name="sinkhorn",
    )(snapshots, coefficients)


def solution(mesh):
    placed = (P("tm", None, "space", None), P(None, "space", None))
    return jax.shard_map(
        per_device,
        mesh=mesh,
        in_specs=placed,
        out_specs=(P("tm", None, "space", None), P("tm", None, "space", None)),
        check_vma=False,
    )
```

```python
import jax
import jax.numpy as jnp
from jax import lax
from jax.experimental import pallas as pl
from jax.experimental.pallas import tpu as pltpu
from jax.sharding import PartitionSpec as P

MESH = pl.DeviceIdType.MESH
TILE = 8
LANES = 128
PAD = 2 * TILE
GROUP = 3
SPAN = GROUP * TILE
STOP = 3
OWN = 3
GO = 1
GO_STEP = 3
TAU_ROWS = 0.25
TAU_SIDE = 0.125


def body(
    tm,
    space,
    snap,
    coef,
    u_out,
    v_out,
    a_ext,
    b_ext,
    c_ext,
    c_str,
    a_str,
    b_str,
    ones,
    first_u,
    first_v,
    second_u,
    second_v,
    mid_a,
    mid_b,
    recip,
    row_b,
    side_b,
    row_d,
    side_d,
    g_row,
    g_right,
    g_left,
    keep,
    g_pl,
    hop,
    loc_sem,
    snd,
    rcv,
    hop_snd,
    hop_rcv,
    on_snd,
    ready,
    ready_via,
    ready_go,
    go,
):
    t, s = lax.axis_index("tm"), lax.axis_index("space")
    ahead, behind = lax.rem(t + 1, tm), lax.rem(t + tm - 1, tm)
    has_up, has_dn = s > 0, s < space - 1
    up, dn = jnp.maximum(s - 1, 0), jnp.minimum(s + 1, space - 1)
    height, width = coef.shape[1], coef.shape[2]
    cols = width // LANES
    tiles = height // TILE + 2
    sweep = tiles // GROUP
    steps = height // SPAN
    both = [(p, j) for p in range(2) for j in range(cols)]

    load_c = pltpu.make_async_copy(coef, c_ext.at[:, pl.ds(TILE, height)], loc_sem.at[0])
    load_a = pltpu.make_async_copy(snap.at[0], a_ext.at[:, pl.ds(TILE, height)], loc_sem.at[1])

    half = tm // 2
    stop = 2 * max(1, half // 2 * STOP // 16)
    place = lax.rem(t, half)
    is_src, is_via, is_dst = place == 0, place == stop, place == half - 1

    def ahead_by(n):
        return lax.rem(t + (n + tm) % tm, tm)

    t_partner, t_via, t_far_via = ahead_by(half), ahead_by(stop), ahead_by(half + stop)

    barrier = pltpu.get_barrier_semaphore()

    def tell(sem, dst_t, dst_s):
        pl.semaphore_signal(sem, inc=1, device_id={"tm": dst_t, "space": dst_s}, device_id_type=MESH)

    @pl.when(has_up)
    def _():
        tell(barrier, t, up)

    @pl.when(has_dn)
    def _():
        tell(barrier, t, dn)

    @pl.when(jnp.logical_not(is_dst))
    def _():
        tell(barrier, ahead, s)

        @pl.when(has_up)
        def _():
            tell(barrier, ahead, up)

        @pl.when(has_dn)
        def _():
            tell(barrier, ahead, dn)

    @pl.when(is_src)
    def _():
        tell(barrier, t_partner, s)
        tell(barrier, t_via, s)
        tell(barrier, t_far_via, s)
        tell(barrier, ahead_by(half - 1), s)

    @pl.when(is_via)
    def _():
        tell(barrier, ahead_by(half - 1 - stop), s)

    load_c.start()
    load_a.start()
    beside = has_up.astype(jnp.int32) + has_dn.astype(jnp.int32)
    before = jnp.where(is_src, 1, 1 + beside)
    on_way = jnp.where(jnp.logical_or(is_dst, is_via), 2, 0)
    pl.semaphore_wait(barrier, beside + before + on_way)

    @pl.when(is_via)
    def _():
        tell(ready_via, ahead_by(half - stop), s)
        tell(ready_go, ahead_by(-stop), s)

    @pl.when(is_dst)
    def _():
        tell(ready, ahead_by(1 - half), s)
        tell(ready, ahead_by(1 - half + stop), s)

    def send(i, src, dst, dst_t, dst_s, sent=None):
        return pltpu.make_async_remote_copy(
            src_ref=src,
            dst_ref=dst,
            send_sem=snd.at[i if sent is None else sent],
            recv_sem=rcv.at[i],
            device_id={"tm": dst_t, "space": dst_s},
            device_id_type=MESH,
        )

    first, last = pl.ds(TILE, TILE), pl.ds(height, TILE)
    head, tail = pl.ds(0, TILE), pl.ds(height + TILE, TILE)
    to_up = [
        send(0, c_ext.at[:, first], c_ext.at[:, tail], t, up),
        send(1, a_ext.at[:, first], a_ext.at[:, tail], t, up),
        send(2, a_ext.at[:, first], b_ext.at[:, tail], behind, up),
    ]
    to_dn = [
        send(3, c_ext.at[:, last], c_ext.at[:, head], t, dn),
        send(4, a_ext.at[:, last], a_ext.at[:, head], t, dn),
        send(5, a_ext.at[:, last], b_ext.at[:, head], behind, dn),
    ]

    b_beside = [
        send(2, b_ext.at[:, first], b_ext.at[:, tail], t, up, 6 + steps),
        send(5, b_ext.at[:, last], b_ext.at[:, head], t, dn, 7 + steps),
    ]

    def part(k, size):
        rows = pl.ds(k * SPAN + TILE, size)
        return send(6 + k, a_ext.at[:, rows], b_ext.at[:, rows], behind, s)

    parts = [part(k, SPAN if k < steps - 1 else height - k * SPAN) for k in range(steps)]

    def start_beside(n):
        @pl.when(has_up)
        def _():
            to_up[n].start()

        @pl.when(has_dn)
        def _():
            to_dn[n].start()

    load_c.wait()
    start_beside(0)
    load_a.wait()
    start_beside(1)

    @pl.when(jnp.logical_not(is_src))
    def _():
        start_beside(2)
        for copy in parts:
            copy.start()

    def legs(k, n):
        lo, size = k * SPAN + TILE, SPAN
        if k == steps:
            lo, size = height, TILE
        src, dst, dst_t, sent = (
            (a_ext, hop, t_partner, hop_snd),
            (a_ext, hop, t_far_via, hop_snd),
            (hop, b_ext, ahead_by(half - 1), on_snd),
            (hop, b_ext, ahead_by(half - 1 - stop), on_snd),
        )[n]
        rows = pl.ds(lo, size)
        return pltpu.make_async_remote_copy(
            src_ref=src.at[:, rows],
            dst_ref=dst.at[:, rows],
            send_sem=sent.at[k],
            recv_sem=hop_rcv.at[k],
            device_id={"tm": dst_t, "space": s},
            device_id_type=MESH,
        )

    own, by_via = (steps, *range(OWN)), range(OWN, steps)

    @pl.when(is_src)
    def _():
        for k in own:
            legs(k, 0).start()

    def pass_on(here, chunks, n):
        @pl.when(here)
        def _():
            pl.semaphore_wait(ready, 1)
            for k in chunks:
                legs(k, n).wait_recv()
                legs(k, n).start()

    def arrived(k):
        @pl.when(is_dst)
        def _():
            if k:
                legs(k, 2).wait_recv()

        @pl.when(jnp.logical_not(is_dst))
        def _():
            parts[k].wait_recv()

    def halo_arrived(n):
        @pl.when(has_up)
        def _():
            to_dn[n].wait_recv()

        @pl.when(has_dn)
        def _():
            to_up[n].wait_recv()

    lane = lax.broadcasted_iota(jnp.int32, (TILE, LANES), 1)
    is_first, is_last = lane == 0, lane == LANES - 1
    zeros = jnp.zeros((TILE, LANES), jnp.float32)

    def at(row, shift=0):
        return pl.ds(row + (PAD + shift), TILE)

    def tile(e):
        return pl.ds(pl.multiple_of(TILE * e, TILE), TILE)

    def clear_top(ref):
        @pl.when(jnp.logical_not(has_up))
        def _():
            for p, j in both:
                ref[p, j, at(0), :] = zeros

    def clear_end(ref):
        @pl.when(jnp.logical_not(has_dn))
        def _():
            for p, j in both:
                ref[p, j, at(height + TILE), :] = zeros

    def from_right(x, j):
        return pltpu.roll(jnp.where(is_first, x[(j + 1) % cols], x[j]), LANES - 1, 1)

    def from_left(x, j):
        return pltpu.roll(jnp.where(is_last, x[j - 1], x[j]), 1, 1)

    def row_pass(src, p, j, row):
        mid = src[p, j, at(row), :]
        below = g_row[p, j, at(row), :] * (src[p, j, at(row, 1), :] - mid)
        above = g_row[p, j, at(row, -1), :] * (mid - src[p, j, at(row, -1), :])
        return mid + (below - above)

    def side_pass(src, dst, row):
        for p in range(2):
            for j in range(cols):
                mid = src[p, j, at(row), :]
                right = jnp.where(is_first, src[p, (j + 1) % cols, at(row), :], mid)
                left = jnp.where(is_last, src[p, (j - 1) % cols, at(row), :], mid)
                dst[p, j, at(row), :] = (
                    keep[p, j, at(row), :] * mid + g_pl[j, at(row), :] * src[1 - p, j, at(row), :]
                ) + (
                    g_right[p, j, at(row), :] * pltpu.roll(right, LANES - 1, 1)
                    + g_left[p, j, at(row), :] * pltpu.roll(left, 1, 1)
                )

    def first_three(*runs):
        for src, row_tmp, _, _, rows in runs:
            for r in rows:
                for p, j in both:
                    row_tmp[p, j, at(r), :] = row_pass(src, p, j, r)
        for _, row_tmp, side_tmp, _, rows in runs:
            for r in rows:
                side_pass(row_tmp, side_tmp, r)
        for _, _, side_tmp, dst, rows in runs:
            for r in rows:
                side_pass(side_tmp, dst, r)

    def run(row, n):
        return [row + TILE * i for i in range(n)]

    def fourth(src, num, dst, row, n=GROUP):
        for i in range(n):
            r = row + TILE * i
            for p, j in both:
                den = row_pass(src, p, j, r)
                dst[p, j, at(r), :] = (1.0 if num is None else num[p, j, at(r), :]) / den

    def strip(src, dst, e):
        for p, j in both:
            dst[p, j, at(TILE * e), :] = src[p, tile(e), pl.ds(LANES * j, LANES)]

    def weigh(e):
        row = TILE * e
        c = [[c_str[p, j, at(row), :] for j in range(cols)] for p in range(2)]
        for j in range(cols):
            g_pl[j, at(row), :] = (0.5 * TAU_SIDE) * (c[0][j] + c[1][j])
        for p in range(2):
            walls = [(0.5 * TAU_SIDE) * c[p][j] for j in range(cols)]
            right = [walls[j] + from_right(walls, j) for j in range(cols)]
            right[-1] = jnp.where(is_last, 0.0, right[-1])
            for j in range(cols):
                left = from_left(right, j)
                kept = 1.0 - walls[j] - (0.5 * TAU_SIDE) * (c[0][j] + c[1][j]) - right[j] - left
                if j == 0:
                    kept = jnp.where(is_first, kept - walls[j], kept)
                if j == cols - 1:
                    kept = jnp.where(is_last, kept - walls[j], kept)
                g_right[p, j, at(row), :] = right[j]
                g_left[p, j, at(row), :] = left
                keep[p, j, at(row), :] = kept
                g_row[p, j, at(row), :] = (0.5 * TAU_ROWS) * (c[p][j] + c_str[p, j, at(row, 1), :])

    @pl.loop(0, tiles)
    def _(e):
        for p, j in both:
            ones[p, j, at(TILE * e), :] = zeros + 1.0

    clear_top(ones)
    clear_end(ones)
    @pl.loop(1, tiles - 1)
    def _(e):
        strip(c_ext, c_str, e)

    @pl.loop(1, tiles - 1, unroll=2)
    def _(e):
        weigh(e)

    inner = sweep - 1
    gap = (tiles * TILE - inner * SPAN) // 2

    @pl.loop(0, GROUP)
    def _(g):
        first_three((ones, row_b, side_b, mid_a, run(gap + TILE * inner * g, inner)))

    @pl.loop(1, tiles - 1)
    def _(e):
        strip(a_ext, a_str, e)

    halo_arrived(0)

    @pl.when(jnp.logical_not(has_up))
    def _():
        c_ext[:, head, :] = jnp.zeros((2, TILE, width), jnp.float32)

    @pl.when(jnp.logical_not(has_dn))
    def _():
        c_ext[:, tail, :] = jnp.zeros((2, TILE, width), jnp.float32)

    for e in (0, tiles - 1):
        strip(c_ext, c_str, e)
    for e in (0, tiles - 2, tiles - 1):
        weigh(e)
    first_three((ones, row_b, side_b, mid_a, run(gap - SPAN, GROUP) + run(tiles * TILE - gap, GROUP)))
    clear_top(mid_a)
    clear_end(mid_a)
    halo_arrived(1)

    for e in (0, tiles - 1):
        strip(a_ext, a_str, e)

    @pl.loop(0, sweep)
    def _(g):
        fourth(mid_a, a_str, first_u, SPAN * g)

    clear_top(first_u)
    clear_end(first_u)

    @pl.when(is_src)
    def _():
        pl.semaphore_wait(ready_via, 1)
        for k in by_via:
            legs(k, 1).start()

    @pl.loop(0, GROUP)
    def _(g):
        first_three((first_u, row_b, side_b, mid_b, run(TILE * sweep * g, sweep)))

    clear_top(mid_b)
    clear_end(mid_b)
    pass_on(is_src, own, 2)

    @pl.loop(0, sweep)
    def _(g):
        fourth(mid_b, None, recip, SPAN * g)

    def scale(e, n):
        for i in range(n):
            for p, j in both:
                b = b_ext[p, tile(e + i), pl.ds(LANES * j, LANES)]
                b_str[p, j, at(TILE * (e + i)), :] = b
                first_v[p, j, at(TILE * (e + i)), :] = b * recip[p, j, at(TILE * (e + i)), :]

    ends = [SPAN * k + (SPAN + 4) for k in range(steps - 1)] + [height + TILE]
    sizes = [GROUP] * (steps - 1) + [tiles - 1 - GROUP * (steps - 1)]

    def run_b(k):
        n = sizes[k] + (k == 0)
        return first_v, row_b, side_b, mid_a, run(ends[k] + 3 - TILE * n, n)

    def run_d(k):
        return second_u, row_d, side_d, mid_b, run(ends[k] + 1 - TILE * sizes[k], sizes[k])

    def clear(k, ref):
        if k == 0:
            clear_top(ref)
        if k == steps - 1:
            clear_end(ref)

    def give(src, out, lo, hi):
        for e in range(lo, hi):
            for p, j in both:
                out[0, p, pl.ds(TILE * (e - 1), TILE), pl.ds(LANES * j, LANES)] = src[p, j, at(TILE * e), :]

    def done(k):
        return tiles - 1 if k == steps - 1 else GROUP * (k + 1)

    def finish(k):
        clear(k, mid_b)
        fourth(mid_b, b_str, second_v, ends[k] - TILE * sizes[k], sizes[k])
        give(second_v, v_out, done(k - 1) if k else 1, done(k))

    def step(k):
        scale(0 if k == 0 else GROUP * k + 1, sizes[k] + (k == 0))
        clear(k, first_v)
        if k == 0:
            first_three(run_b(k))
        else:
            first_three(run_b(k), run_d(k - 1))
        clear(k, mid_a)
        fourth(mid_a, a_str, second_u, ends[k] + 2 - TILE * sizes[k], sizes[k])
        clear(k, second_u)
        give(second_u, u_out, done(k - 1) if k else 1, done(k))
        if k:
            finish(k - 1)

    @pl.when(is_dst)
    def _():
        legs(steps, 2).wait_recv()

        @pl.when(has_dn)
        def _():
            b_beside[1].start()

        legs(0, 2).wait_recv()

        @pl.when(has_up)
        def _():
            b_beside[0].start()

    halo_arrived(2)

    for k in range(steps):
        arrived(k)
        if k == GO_STEP:

            @pl.when(is_src)
            def _():
                for n in own[: GO + 1]:
                    legs(n, 2).wait_send()
                pl.semaphore_wait(ready_go, 1)
                tell(go, t_via, s)

        step(k)

    first_three(run_d(steps - 1))
    finish(steps - 1)

    @pl.when(is_via)
    def _():
        pl.semaphore_wait(go, 1)

    pass_on(is_via, by_via, 3)

    for n in range(3):

        @pl.when(has_up if n < 2 else jnp.logical_and(has_up, jnp.logical_not(is_src)))
        def _():
            to_up[n].wait_send()

        @pl.when(has_dn if n < 2 else jnp.logical_and(has_dn, jnp.logical_not(is_src)))
        def _():
            to_dn[n].wait_send()

    @pl.when(jnp.logical_not(is_src))
    def _():
        for copy in parts:
            copy.wait_send()

    @pl.when(jnp.logical_and(is_dst, has_up))
    def _():
        b_beside[0].wait_send()

    @pl.when(jnp.logical_and(is_dst, has_dn))
    def _():
        b_beside[1].wait_send()

    for here, chunks, n in (
        (is_src, own, 0),
        (is_src, by_via, 1),
        (is_src, own[GO + 1 :], 2),
        (is_via, by_via, 3),
    ):

        @pl.when(here)
        def _():
            for k in chunks:
                legs(k, n).wait_send()


def per_device(snapshots, coefficients):
    tm, space = lax.axis_size("tm"), lax.axis_size("space")
    planes, height, width = coefficients.shape
    cols = width // LANES
    rows = height + 2 * TILE
    wide = (planes, rows, width)
    field = pltpu.VMEM((planes, cols, rows + 2 * PAD, LANES), jnp.float32)
    copies = 8 + rows // SPAN

    def kernel(*refs):
        body(tm, space, *refs)

    return pl.pallas_call(
        kernel,
        out_shape=[jax.ShapeDtypeStruct(snapshots.shape, jnp.float32)] * 2,
        in_specs=[pl.BlockSpec(memory_space=pltpu.HBM)] * 2,
        out_specs=[pl.BlockSpec(memory_space=pltpu.VMEM)] * 2,
        scratch_shapes=[pltpu.VMEM(wide, jnp.float32)] * 3
        + [field] * 19
        + [pltpu.VMEM((cols, rows + 2 * PAD, LANES), jnp.float32)]
        + [pltpu.VMEM(wide, jnp.float32)]
        + [pltpu.SemaphoreType.DMA((2,)), pltpu.SemaphoreType.DMA((copies,)), pltpu.SemaphoreType.DMA((copies,))]
        + [pltpu.SemaphoreType.DMA((rows // SPAN + 1,))] * 3
        + [pltpu.SemaphoreType.REGULAR] * 4,
        compiler_params=pltpu.CompilerParams(collective_id=0, has_side_effects=True, vmem_limit_bytes=51 * 2**20),
        name="sinkhorn",
    )(snapshots, coefficients)


def solution(mesh):
    placed = (P("tm", None, "space", None), P(None, "space", None))
    return jax.shard_map(
        per_device,
        mesh=mesh,
        in_specs=placed,
        out_specs=(P("tm", None, "space", None), P("tm", None, "space", None)),
        check_vma=False,
    )
```
